32 devices in a mesh: seq: 16 (over z, y, x), tp: 2 (over core).
Axes of the slice: x: 2, y: 2, z: 4, core: 2. Of those that a mesh axis runs over, the one named last changes fastest.
Arguments:
- queries: bfloat16 [4096, 8192], P('seq', 'tp'), may hold values from -24 to 24
- keys: bfloat16 [4096, 1024], P('seq', 'tp'), may hold values from -24 to 24
- values: bfloat16 [4096, 1024], P('seq', 'tp'), may hold values from -500 to 500
- doc_ids: int32 [4096], P('seq'), may hold values from 0 to 3, never falling along the last dimension, each value on 1 to 2048 neighbouring positions
- features: bfloat16 [2048, 4096], P('seq'), may hold values from -6 to 6
- projector: bfloat16 [4096, 8192], P('seq', 'tp'), may hold values from -6 to 6
- span_start: int32 [2048], P('seq'), may hold values from 0 to 4092, as said below
- span_len: int32 [2048], P('seq'), may hold values from 1 to 4
- counts: int32 [16], replicated, may hold values from 64 to 128
Outputs:
- targets: bfloat16 [2048, 8192], P('seq', 'tp')
- projector_new: float32 [4096, 8192], P('seq', 'tp')
The draws below stay inside these ranges and needn't reach their ends.
Inputs may be any that keep to these rules, and one draw needn't show every extreme that they name: `span_start`: slots d * 128 to (d + 1) * 128 - 1 belong to index d of seq and the first counts[d] of them are live. Live starts increase within an index and lie in teacher rows d * 256 to (d + 1) * 256 - 1; a live span ends at most 3 rows past that block and never past row 4095. Slots that are not live hold start d * 256 and length 1.
All inputs are finite; a program needn't handle non-finite values.
Results may differ from the reference program's by a relative error of at most 0.017.
Values may be sent and summed in bfloat16 or wider, within the bound.
A program may use at most 192 MiB of HBM per device.

```python
import math
import jax
import jax.numpy as jnp
import numpy as np
from jax import lax

H = 64
KVH = 8
HD = 128
DS = 4096
TT_DEV = 256
MAXSPAN = 4
SCAP = 128
DT = 8192
TT = 4096
SLOTS = 2048
DOC_MOST = 2048
N_SEQ = 16


def attention_base(key):
    base_keys = jnp.clip(jax.random.normal(key, (TT, KVH, HD), jnp.float32), -4.0, 4.0)
    return base_keys


def span_plan(key):
    key = jax.random.fold_in(key, 31)
    devices = jnp.arange(N_SEQ, dtype=jnp.int32)
    counts = jax.random.randint(jax.random.fold_in(key, 1), (N_SEQ,), SCAP // 2, SCAP + 1).astype(jnp.int32)
    full_device = jax.random.randint(jax.random.fold_in(key, 2), (), 0, N_SEQ).astype(jnp.int32)
    low_device = (full_device + jax.random.randint(jax.random.fold_in(key, 3), (), 1, N_SEQ).astype(jnp.int32)) % N_SEQ
    counts = jnp.where(devices == full_device, SCAP, jnp.where(devices == low_device, SCAP // 2, counts)).astype(jnp.int32)
    free_room = TT_DEV - MAXSPAN
    shuffled = jax.vmap(lambda subkey: jax.random.permutation(subkey, free_room))(jax.random.split(jax.random.fold_in(key, 4), N_SEQ)).astype(jnp.int32)
    chosen = shuffled < counts[:, None] - 1
    ordered = jnp.argsort(jnp.where(chosen, 0, 1).astype(jnp.int32), axis=1, stable=True)[:, :SCAP].astype(jnp.int32)
    slot_ids = jnp.arange(SCAP, dtype=jnp.int32)[None, :]
    live_count = counts[:, None]
    last_offset = jnp.where(devices == N_SEQ - 1, TT_DEV - MAXSPAN, TT_DEV - 1).astype(jnp.int32)[:, None]
    offsets = jnp.where(slot_ids < live_count - 1, ordered, jnp.where(slot_ids == live_count - 1, last_offset, 0))
    drawn_len = jax.random.randint(jax.random.fold_in(key, 5), (N_SEQ, SCAP), 1, MAXSPAN + 1).astype(jnp.int32)
    lengths = jnp.where(slot_ids < live_count - 1, drawn_len, jnp.where(slot_ids == live_count - 1, MAXSPAN, 1))
    starts = devices[:, None] * TT_DEV + offsets
    return (counts, starts.reshape(-1).astype(jnp.int32), lengths.reshape(-1).astype(jnp.int32))


def draw_keys(key, part):
    base_keys = attention_base(key)
    return base_keys.reshape(TT, KVH * HD).astype(jnp.bfloat16)


def draw_queries(key, part):
    key = jax.random.fold_in(key, 12)
    own_queries = jnp.clip(jax.random.normal(key, (TT, KVH, H // KVH, HD), jnp.float32), -4.0, 4.0)
    return own_queries.reshape(TT, H * HD).astype(jnp.bfloat16)


def draw_values(key, part):
    key = jax.random.fold_in(key, 13)
    head_rank = jnp.arange(KVH, dtype=jnp.float32)[None, :, None] / max(KVH - 1, 1)
    tokens = jnp.exp(jax.random.uniform(jax.random.fold_in(key, 1), (TT, 1, 1), jnp.float32, 0.0, math.log(4.0)))
    random_part = jnp.clip(jax.random.normal(key, (TT, KVH, HD), jnp.float32), -4.0, 4.0)
    return (random_part * 10.0 ** head_rank * tokens).reshape(TT, KVH * HD).astype(jnp.bfloat16)


def draw_span_start(key, part):
    plan = span_plan(key)
    return plan[1]


def draw_span_len(key, part):
    plan = span_plan(key)
    return plan[2]


def draw_counts(key, part):
    plan = span_plan(key)
    return plan[0]


def block_levels(rng, extent, pieces, smallest, largest):
    def one(position, blocks):
        steps = jax.random.uniform(jax.random.fold_in(jax.random.fold_in(rng, 6), position), (blocks,), jnp.float32, smallest / len(pieces), largest / len(pieces))
        return jnp.repeat(jnp.exp(steps), extent[position] // blocks).reshape((-1,) + (1,) * (len(extent) - position - 1))

    level = one(*pieces[0])
    for cut in pieces[1:]:
        level = level * one(*cut)
    return level


def profile(count, total, reach, lean):
    portions = [(1 << 20) // math.isqrt(rank ** lean) + 1 for rank in range(2, count + 1)]
    rest, given = total - reach - (count - 1), [1] * (count - 1)
    while rest > 0:
        movable = [i for i in range(count - 1) if given[i] < reach]
        mass, budget = sum([portions[i] for i in movable]), rest
        for i in movable:
            more = min(reach - given[i], max(1, budget * portions[i] // mass), rest)
            given[i] = given[i] + more
            rest = rest - more
    return np.array([reach] + given)


def ragged_sizes(stream_key, number_of, total, most, skew):
    if number_of == 2:
        one = jax.random.randint(stream_key, (), max(1, total - most), min(most, total - 1) + 1)
        return jnp.stack([one, total - one])
    tallies = jnp.asarray(profile(number_of, total, most, skew), jnp.int32)
    pairs = (number_of - 1) // 2
    donor, sink = tallies[1:1 + 2 * pairs:2], tallies[2:2 + 2 * pairs:2]
    room = jnp.minimum(donor - 1, most - sink)
    shifted = jax.random.randint(jax.random.fold_in(stream_key, 1), (pairs,), 0, 1 << 20) % (room + 1)
    tallies = tallies.at[1:1 + 2 * pairs:2].set(donor - shifted).at[2:2 + 2 * pairs:2].set(sink + shifted)
    return tallies[jax.random.permutation(jax.random.fold_in(stream_key, 2), number_of)]


def centred(rng, extent, deviation, most, cuts=(), kind=jnp.bfloat16):
    array = jax.random.normal(rng, extent, jnp.float32) * deviation
    if len(cuts) > 0:
        array = block_levels(rng, extent, cuts, -0.22, 0.18) * array
    return jnp.clip(array, min=-most, max=most).astype(kind)


def setup_inputs(seed: int = 0) -> dict:
    seeds = jax.random.split(jax.random.key(seed), 10)
    return {
        "queries": draw_queries(jax.random.fold_in(seeds[9], 71), 0),
        "keys": draw_keys(jax.random.fold_in(seeds[9], 71), 0),
        "values": draw_values(jax.random.fold_in(seeds[9], 71), 0),
        "doc_ids": jnp.searchsorted(jnp.cumsum(ragged_sizes(seeds[3], N_SEQ // 4, TT, DOC_MOST, 2)), jnp.arange(TT), side="right").astype(jnp.int32),
        "features": centred(seeds[4], (SLOTS, DS), 1.0, 6.0, ((0, 16),)),
        "projector": centred(seeds[5], (DS, DT), 1.0, 6.0, ((0, 16), (1, 2))),
        "span_start": draw_span_start(jax.random.fold_in(seeds[9], 71), 0),
        "span_len": draw_span_len(jax.random.fold_in(seeds[9], 71), 0),
        "counts": draw_counts(jax.random.fold_in(seeds[9], 71), 0),
    }


eta_step = 0.5
ridge_weight = 0.1
norm_eps = 1e-06
neg_large = -1e+30

def attention_block(block_index, queries, keys, values, doc_ids):
    groups = H // KVH
    first_row = block_index * TT_DEV
    key_grid = keys.reshape(TT, KVH, HD).astype(jnp.float32)
    value_grid = values.reshape(TT, KVH, HD).astype(jnp.float32)
    query_grid = lax.dynamic_slice_in_dim(queries, first_row, TT_DEV, 0).reshape(TT_DEV, KVH, groups, HD).astype(jnp.float32)
    query_pos = first_row + jnp.arange(TT_DEV, dtype=jnp.int32)
    query_doc = lax.dynamic_slice_in_dim(doc_ids, first_row, TT_DEV, 0)
    key_pos = jnp.arange(TT, dtype=jnp.int32)
    visible = (doc_ids[None, :] == query_doc[:, None]) & (key_pos[None, :] <= query_pos[:, None])
    scores = jnp.einsum('tkgd,ukd->kgtu', query_grid, key_grid) / math.sqrt(HD)
    scores = jnp.where(visible, scores, neg_large)
    row_max = lax.optimization_barrier(jnp.max(scores, axis=3, keepdims=True))
    probs = jnp.where(visible, jnp.exp(scores - row_max), 0.0)
    sums = lax.optimization_barrier(jnp.sum(probs, axis=3))
    probs_low = lax.optimization_barrier(probs.astype(jnp.bfloat16)).astype(jnp.float32)
    mixed = jnp.einsum('kgtu,ukd->kgtd', probs_low, value_grid) / sums[..., None]
    return mixed.transpose(2, 0, 1, 3).reshape(TT_DEV, H * HD).astype(jnp.bfloat16)

def reference(queries, keys, values, doc_ids, features, projector, span_start, span_len, counts):
    block_ids = jnp.arange(N_SEQ, dtype=jnp.int32)
    attn_out = lax.map(lambda block_index: attention_block(block_index, queries, keys, values, doc_ids), block_ids)
    attn_out = attn_out.reshape(TT, H * HD)
    padded = jnp.concatenate([attn_out, jnp.zeros((MAXSPAN - 1, H * HD), jnp.bfloat16)], axis=0)

    def span_block(block_index):
        extended = lax.dynamic_slice_in_dim(padded, block_index * TT_DEV, TT_DEV + MAXSPAN - 1, 0)
        offsets = lax.dynamic_slice_in_dim(span_start, block_index * SCAP, SCAP, 0) - block_index * TT_DEV
        lengths = lax.dynamic_slice_in_dim(span_len, block_index * SCAP, SCAP, 0)
        columns = jnp.arange(TT_DEV + MAXSPAN - 1, dtype=jnp.int32)
        one_hot = ((columns[None, :] >= offsets[:, None]) & (columns[None, :] < (offsets + lengths)[:, None])).astype(jnp.bfloat16)
        return jnp.dot(one_hot, extended, preferred_element_type=jnp.float32)
    span_sum = lax.map(span_block, block_ids).reshape(SLOTS, H * HD)
    slot_ids = jnp.arange(SLOTS, dtype=jnp.int32)
    is_live = slot_ids % SCAP < counts[slot_ids // SCAP]
    span_mean = jnp.where(is_live[:, None], span_sum / span_len[:, None].astype(jnp.float32), 0.0)
    mean_sq = lax.optimization_barrier(jnp.mean(span_mean * span_mean, axis=1))
    targets = (span_mean * lax.rsqrt(mean_sq + norm_eps)[:, None]).astype(jnp.bfloat16)
    prediction = jnp.dot(features, projector, preferred_element_type=jnp.float32) / math.sqrt(DS)
    errors = jnp.where(is_live[:, None], targets.astype(jnp.float32) - prediction, 0.0).astype(jnp.bfloat16)

    def add_block(carried, block_index):
        feature_rows = lax.dynamic_slice_in_dim(features, block_index * SCAP, SCAP, 0)
        error_rows = lax.dynamic_slice_in_dim(errors, block_index * SCAP, SCAP, 0)
        gram_term = lax.dot_general(feature_rows, error_rows, (((0,), (0,)), ((), ())), preferred_element_type=jnp.float32)
        return (carried + lax.optimization_barrier(gram_term.astype(jnp.bfloat16)).astype(jnp.float32), None)
    gram_sum, _ = lax.scan(add_block, jnp.zeros((DS, H * HD), jnp.float32), block_ids)
    live_total = jnp.sum(counts).astype(jnp.float32)
    projector_wide = projector.astype(jnp.float32)
    projector_new = projector_wide + eta_step * (math.sqrt(DS) * gram_sum / live_total - ridge_weight * projector_wide)
    return (targets, projector_new)
```

```python
import functools
import math

import jax
import jax.numpy as jnp
from jax import lax
from jax.experimental import pallas as pl
from jax.experimental.pallas import tpu as pltpu
from jax.sharding import PartitionSpec as P

HD = 128
MAXSPAN = 4
RIM = 16

eta_step = 0.5
ridge_weight = 0.1
norm_eps = 1e-06
neg_large = -1e30

NT = (((1,), (1,)), ((), ()))


def attention_kernel(groups, spot_ref, q_ref, k_ref, vt_ref, start_ref, hot_ref, out_ref,
                     acc, top, total, bias):
    own = spot_ref[0]
    lowest = spot_ref[1]
    tok = q_ref.shape[0]
    rate = HD ** (-0.5) * math.log2(math.e)
    top[...] = jnp.full(top.shape, neg_large, jnp.float32)
    total[...] = jnp.zeros(total.shape, jnp.float32)
    acc[...] = jnp.zeros(acc.shape, jnp.float32)
    query_pos = own * tok + lax.broadcasted_iota(jnp.int32, (tok, tok), 1)

    def advance(step, carry):
        block = own - step
        key_pos = block * tok + lax.broadcasted_iota(jnp.int32, (tok, tok), 0)
        visible = (key_pos >= start_ref[...]) & (key_pos <= query_pos)
        bias[...] = jnp.where(visible, 0.0, neg_large)
        key_block = k_ref[block]
        value_block = vt_ref[block]
        for g in range(groups):
            lanes = slice(g * HD, (g + 1) * HD)
            scores = lax.dot_general(
                key_block, q_ref[:, lanes], NT, preferred_element_type=jnp.float32
            ) + bias[...]
            old_top = top[g:g + 1, :]
            new_top = jnp.maximum(old_top, jnp.max(scores, axis=0, keepdims=True))
            weights = jnp.exp2((scores - new_top) * rate)
            factor = jnp.exp2((old_top - new_top) * rate)
            top[g:g + 1, :] = new_top
            total[g:g + 1, :] = total[g:g + 1, :] * factor + jnp.sum(
                weights, axis=0, keepdims=True
            )
            acc[lanes, :] = acc[lanes, :] * factor + jnp.dot(
                value_block, weights.astype(jnp.bfloat16), preferred_element_type=jnp.float32
            )
        return carry

    lax.fori_loop(0, own - lowest + 1, advance, 0)
    for g in range(groups):
        lanes = slice(g * HD, (g + 1) * HD)
        mixed = (acc[lanes, :] / total[g:g + 1, :]).astype(jnp.bfloat16)
        out_ref[:, lanes] = lax.dot_general(
            hot_ref[...], mixed, NT, preferred_element_type=jnp.float32
        )


def attend(spot, queries, key_blocks, value_blocks, doc_start, one_hot, kv_heads, groups):
    tok = queries.shape[0]
    count = key_blocks.shape[0]
    hot_rows = one_hot.shape[0]
    wide = groups * HD
    return pl.pallas_call(
        functools.partial(attention_kernel, groups),
        out_shape=jax.ShapeDtypeStruct((hot_rows, queries.shape[1]), jnp.float32),
        grid_spec=pltpu.PrefetchScalarGridSpec(
            num_scalar_prefetch=1,
            grid=(kv_heads,),
            in_specs=[
                pl.BlockSpec((tok, wide), lambda i, s: (0, i)),
                pl.BlockSpec((count, tok, HD), lambda i, s: (0, 0, i)),
                pl.BlockSpec((count, HD, tok), lambda i, s: (0, i, 0)),
                pl.BlockSpec((1, tok), lambda i, s: (0, 0)),
                pl.BlockSpec((hot_rows, tok), lambda i, s: (0, 0)),
            ],
            out_specs=pl.BlockSpec((hot_rows, wide), lambda i, s: (0, i)),
            scratch_shapes=[
                pltpu.VMEM((wide, tok), jnp.float32),
                pltpu.VMEM((groups, tok), jnp.float32),
                pltpu.VMEM((groups, tok), jnp.float32),
                pltpu.VMEM((tok, tok), jnp.float32),
            ],
        ),
        compiler_params=pltpu.CompilerParams(vmem_limit_bytes=40 * 1024 * 1024),
        cost_estimate=pl.CostEstimate(
            flops=4 * tok * queries.shape[1] * 2304,
            bytes_accessed=2 * key_blocks.size * 2 + queries.size * 2,
            transcendentals=tok * queries.shape[1] // HD * 2304,
        ),
    )(spot, queries, key_blocks, value_blocks, doc_start, one_hot)


def shards(queries, keys, values, doc_ids, features, projector, span_start, span_len, counts):
    tok = queries.shape[0]
    kv_heads = keys.shape[1] // HD
    groups = queries.shape[1] // (kv_heads * HD)
    slots = features.shape[0]
    seq_index = lax.axis_index("seq")
    seq_size = lax.axis_size("seq")
    first_row = seq_index * tok

    key_blocks = lax.all_gather(keys, "seq")
    value_blocks = lax.all_gather(values.T, "seq")
    all_docs = lax.all_gather(doc_ids, "seq", axis=0, tiled=True)
    all_features = lax.all_gather(features, "seq", axis=0, tiled=True)
    columns = lax.all_to_all(projector, "seq", split_axis=1, concat_axis=0, tiled=True)

    doc_start = jnp.sum((all_docs[None, :] < doc_ids[:, None]).astype(jnp.int32), axis=1)
    spot = jnp.stack([seq_index.astype(jnp.int32), doc_start[0] // tok])
    offsets = span_start - first_row
    places = jnp.arange(tok + RIM, dtype=jnp.int32)
    one_hot = (
        (places[None, :] >= offsets[:, None]) & (places[None, :] < (offsets + span_len)[:, None])
    ).astype(jnp.bfloat16)
    picks = (jnp.arange(RIM)[:, None] == jnp.arange(tok)[None, :]).astype(jnp.bfloat16)
    hot = jnp.concatenate([one_hot[:, :tok], picks], axis=0)
    pooled = attend(
        spot, queries, key_blocks, value_blocks, doc_start[None, :], hot, kv_heads, groups
    )
    route = [(i + 1, i) for i in range(seq_size - 1)]
    rim = lax.ppermute(pooled[slots:].astype(jnp.bfloat16), "seq", route)
    span_sum = pooled[:slots] + jnp.dot(
        one_hot[:, tok:], rim, preferred_element_type=jnp.float32
    )
    is_live = jnp.arange(slots, dtype=jnp.int32) < lax.dynamic_index_in_dim(
        counts, seq_index, keepdims=False
    )
    span_mean = jnp.where(is_live[:, None], span_sum / span_len[:, None].astype(jnp.float32), 0.0)
    row_sq = lax.psum(jnp.sum(span_mean * span_mean, axis=1), "tp")
    mean_sq = row_sq / (span_mean.shape[1] * lax.axis_size("tp"))
    targets = (span_mean * lax.rsqrt(mean_sq + norm_eps)[:, None]).astype(jnp.bfloat16)

    all_slots = seq_size * slots
    slot_ids = jnp.arange(all_slots, dtype=jnp.int32)
    all_live = slot_ids % slots < jnp.repeat(counts, slots, total_repeat_length=all_slots)
    prediction = jnp.dot(all_features, columns, preferred_element_type=jnp.float32)
    prediction = prediction * features.shape[1] ** (-0.5)
    target_columns = lax.all_to_all(targets, "seq", split_axis=1, concat_axis=0, tiled=True)
    errors = jnp.where(
        all_live[:, None], target_columns.astype(jnp.float32) - prediction, 0.0
    ).astype(jnp.bfloat16)
    gram = lax.dot_general(
        all_features, errors, (((0,), (0,)), ((), ())), preferred_element_type=jnp.float32
    ).astype(jnp.bfloat16)
    gram_sum = lax.all_to_all(gram, "seq", split_axis=0, concat_axis=1, tiled=True)
    live_total = jnp.sum(counts).astype(jnp.float32)
    projector_wide = projector.astype(jnp.float32)
    projector_new = projector_wide + eta_step * (
        math.sqrt(features.shape[1]) * gram_sum.astype(jnp.float32) / live_total
        - ridge_weight * projector_wide
    )
    return (targets, projector_new)


def solution(mesh):
    in_specs = (
        P("seq", "tp"),
        P("seq", "tp"),
        P("seq", "tp"),
        P("seq"),
        P("seq", None),
        P("seq", "tp"),
        P("seq"),
        P("seq"),
        P(),
    )
    out_specs = (P("seq", "tp"), P("seq", "tp"))
    return jax.shard_map(shards, mesh=mesh, in_specs=in_specs, out_specs=out_specs, check_vma=False)
```

```python
import functools
import math

import jax
import jax.numpy as jnp
from jax import lax
from jax.experimental import pallas as pl
from jax.experimental.pallas import tpu as pltpu
from jax.sharding import PartitionSpec as P

HD = 128
MAXSPAN = 4
RIM = 16

eta_step = 0.5
ridge_weight = 0.1
norm_eps = 1e-06
neg_large = -1e30

NT = (((1,), (1,)), ((), ()))


def attention_kernel(groups, spot_ref, q_ref, k_ref, v_ref, start_ref, hot_ref, out_ref,
                     acc, top, total, bias):
    own = spot_ref[0]
    lowest = spot_ref[1]
    tok = q_ref.shape[0]
    rate = HD ** (-0.5) * math.log2(math.e)
    top[...] = jnp.full(top.shape, neg_large, jnp.float32)
    total[...] = jnp.zeros(total.shape, jnp.float32)
    acc[...] = jnp.zeros(acc.shape, jnp.float32)
    query_pos = own * tok + lax.broadcasted_iota(jnp.int32, (tok, tok), 1)

    def advance(step, carry):
        block = own - step
        key_pos = block * tok + lax.broadcasted_iota(jnp.int32, (tok, tok), 0)
        visible = (key_pos >= start_ref[...]) & (key_pos <= query_pos)
        bias[...] = jnp.where(visible, 0.0, neg_large)
        key_block = k_ref[block, :tok, :]
        value_block = v_ref[block, :tok, :].T
        for g in range(groups):
            lanes = slice(g * HD, (g + 1) * HD)
            scores = lax.dot_general(
                key_block, q_ref[:, lanes], NT, preferred_element_type=jnp.float32
            ) + bias[...]
            old_top = top[g:g + 1, :]
            new_top = jnp.maximum(old_top, jnp.max(scores, axis=0, keepdims=True))
            weights = jnp.exp2((scores - new_top) * rate)
            factor = jnp.exp2((old_top - new_top) * rate)
            top[g:g + 1, :] = new_top
            total[g:g + 1, :] = total[g:g + 1, :] * factor + jnp.sum(
                weights, axis=0, keepdims=True
            )
            acc[lanes, :] = acc[lanes, :] * factor + jnp.dot(
                value_block, weights.astype(jnp.bfloat16), preferred_element_type=jnp.float32
            )
        return carry

    lax.fori_loop(0, own - lowest + 1, advance, 0)
    for g in range(groups):
        lanes = slice(g * HD, (g + 1) * HD)
        mixed = (acc[lanes, :] / total[g:g + 1, :]).astype(jnp.bfloat16)
        out_ref[:, lanes] = lax.dot_general(
            hot_ref[...], mixed, NT, preferred_element_type=jnp.float32
        )


def attend(spot, queries, mixed_blocks, doc_start, one_hot, kv_heads, groups):
    tok = queries.shape[0]
    count, rows = mixed_blocks.shape[:2]
    hot_rows = one_hot.shape[0]
    wide = groups * HD
    return pl.pallas_call(
        functools.partial(attention_kernel, groups),
        out_shape=jax.ShapeDtypeStruct((hot_rows, queries.shape[1]), jnp.float32),
        grid_spec=pltpu.PrefetchScalarGridSpec(
            num_scalar_prefetch=1,
            grid=(kv_heads,),
            in_specs=[
                pl.BlockSpec((tok, wide), lambda i, s: (0, i)),
                pl.BlockSpec((count, rows, HD), lambda i, s: (0, 0, i)),
                pl.BlockSpec((count, rows, HD), lambda i, s: (0, 0, i + kv_heads)),
                pl.BlockSpec((1, tok), lambda i, s: (0, 0)),
                pl.BlockSpec((hot_rows, tok), lambda i, s: (0, 0)),
            ],
            out_specs=pl.BlockSpec((hot_rows, wide), lambda i, s: (0, i)),
            scratch_shapes=[
                pltpu.VMEM((wide, tok), jnp.float32),
                pltpu.VMEM((groups, tok), jnp.float32),
                pltpu.VMEM((groups, tok), jnp.float32),
                pltpu.VMEM((tok, tok), jnp.float32),
            ],
        ),
        compiler_params=pltpu.CompilerParams(vmem_limit_bytes=40 * 1024 * 1024),
        cost_estimate=pl.CostEstimate(
            flops=4 * tok * queries.shape[1] * 2304,
            bytes_accessed=mixed_blocks.size * 2 + queries.size * 2,
            transcendentals=tok * queries.shape[1] // HD * 2304,
        ),
    )(spot, queries, mixed_blocks, mixed_blocks, doc_start, one_hot)


def step_kernel(depth, total_ref, old_ref, gram_ref, new_ref):
    wide = old_ref[...].astype(jnp.float32)
    gram = gram_ref[0].astype(jnp.float32)
    rate = eta_step * math.sqrt(depth) / total_ref[...]
    new_ref[...] = wide * (1.0 - eta_step * ridge_weight) + gram * rate


def step(projector, gram_sum, live_total, depth):
    pieces, rows, chunk = gram_sum.shape
    return pl.pallas_call(
        functools.partial(step_kernel, depth),
        out_shape=jax.ShapeDtypeStruct(projector.shape, jnp.float32),
        grid=(pieces,),
        in_specs=[
            pl.BlockSpec((1, 1), lambda i: (0, 0)),
            pl.BlockSpec((rows, chunk), lambda i: (0, i)),
            pl.BlockSpec((1, rows, chunk), lambda i: (i, 0, 0)),
        ],
        out_specs=pl.BlockSpec((rows, chunk), lambda i: (0, i)),
    )(live_total.reshape(1, 1), projector, gram_sum)


def shards(queries, keys, values, doc_ids, features, projector, span_start, span_len, counts):
    tok = queries.shape[0]
    kv_heads = keys.shape[1] // HD
    groups = queries.shape[1] // (kv_heads * HD)
    slots = features.shape[0]
    tok_rows = projector.shape[0]
    seq_index = lax.axis_index("seq")
    seq_size = lax.axis_size("seq")
    first_row = seq_index * tok

    tp_size = lax.axis_size("tp")
    tp_index = lax.axis_index("tp")
    wide = 2 * keys.shape[1]
    doc_rows = jnp.zeros((RIM, wide), jnp.bfloat16)
    doc_rows = lax.dynamic_update_slice(doc_rows, doc_ids.astype(jnp.bfloat16)[None, :], (0, 0))
    mixed = jnp.concatenate([jnp.concatenate([keys, values], axis=1), doc_rows], axis=0)
    mixed_blocks = lax.all_gather(mixed, "seq")
    all_docs = mixed_blocks[:, tok, :tok].reshape(-1).astype(jnp.int32)
    depth = features.shape[1]
    if tp_size == 2:
        half = depth // 2
        part = lax.dynamic_slice_in_dim(features, tp_index * half, half, axis=1)
    else:
        part = features
    part, projector_late, mixed_blocks = lax.optimization_barrier((part, projector, mixed_blocks))
    near = lax.all_gather(part, "seq", axis=0, tiled=True)
    chunk = projector.shape[1] // seq_size
    columns = lax.all_to_all(
        projector_late.reshape(tok_rows, seq_size, chunk).transpose(1, 0, 2), "seq", 0, 0
    ).reshape(depth, chunk)

    doc_start = jnp.sum((all_docs[None, :] < doc_ids[:, None]).astype(jnp.int32), axis=1)
    spot = jnp.stack([seq_index.astype(jnp.int32), doc_start[0] // tok])
    offsets = span_start - first_row
    places = jnp.arange(tok + RIM, dtype=jnp.int32)
    one_hot = (
        (places[None, :] >= offsets[:, None]) & (places[None, :] < (offsets + span_len)[:, None])
    ).astype(jnp.bfloat16)
    picks = (jnp.arange(RIM)[:, None] == jnp.arange(tok)[None, :]).astype(jnp.bfloat16)
    hot = jnp.concatenate([one_hot[:, :tok], picks], axis=0)
    pooled = attend(
        spot, queries, mixed_blocks, doc_start[None, :], hot, kv_heads, groups
    )
    columns, pooled = lax.optimization_barrier((columns, pooled))
    route = [(i + 1, i) for i in range(seq_size - 1)]
    rim = lax.ppermute(pooled[slots:].astype(jnp.bfloat16), "seq", route)
    span_sum = pooled[:slots] + jnp.dot(
        one_hot[:, tok:], rim, preferred_element_type=jnp.float32
    )
    is_live = jnp.arange(slots, dtype=jnp.int32) < lax.dynamic_index_in_dim(
        counts, seq_index, keepdims=False
    )
    span_mean = jnp.where(is_live[:, None], span_sum / span_len[:, None].astype(jnp.float32), 0.0)
    row_sq = lax.psum(jnp.sum(span_mean * span_mean, axis=1), "tp")
    mean_sq = row_sq / (span_mean.shape[1] * lax.axis_size("tp"))
    targets = (span_mean * lax.rsqrt(mean_sq + norm_eps)[:, None]).astype(jnp.bfloat16)

    near, targets_out = lax.optimization_barrier((near, targets))
    all_live = jnp.arange(slots, dtype=jnp.int32)[None, :] < counts[:, None]
    if tp_size == 2:
        far = lax.ppermute(near, "tp", [(0, 1), (1, 0)])
        near_rows = lax.dynamic_slice_in_dim(columns, tp_index * half, half, axis=0)
        far_rows = lax.dynamic_slice_in_dim(columns, (1 - tp_index) * half, half, axis=0)
        prediction = jnp.dot(near, near_rows, preferred_element_type=jnp.float32) + jnp.dot(
            far, far_rows, preferred_element_type=jnp.float32
        )
    else:
        prediction = jnp.dot(near, columns, preferred_element_type=jnp.float32)
    prediction = lax.optimization_barrier(prediction * depth ** (-0.5))
    target_columns = lax.all_to_all(
        targets.reshape(slots, seq_size, chunk).transpose(1, 0, 2), "seq", 0, 0
    )
    errors = jnp.where(
        all_live[:, :, None],
        target_columns.astype(jnp.float32) - prediction.reshape(seq_size, slots, chunk),
        0.0,
    ).astype(jnp.bfloat16)
    errors = lax.optimization_barrier(errors).reshape(seq_size * slots, chunk)
    over_slots = (((0,), (0,)), ((), ()))
    gram = lax.dot_general(near, errors, over_slots, preferred_element_type=jnp.float32).astype(
        jnp.bfloat16
    )
    if tp_size == 2:
        other = lax.dot_general(
            far, errors, over_slots, preferred_element_type=jnp.float32
        ).astype(jnp.bfloat16)
        first = tp_index == 0
        gram = jnp.concatenate([jnp.where(first, gram, other), jnp.where(first, other, gram)], 0)
    gram_sum = lax.all_to_all(gram.reshape(seq_size, tok_rows, chunk), "seq", 0, 0)
    live_total = jnp.sum(counts).astype(jnp.float32)
    if chunk % 128 == 0:
        return (targets_out, step(projector, gram_sum, live_total, depth))
    projector_wide = projector.astype(jnp.float32)
    gram_rows = gram_sum.transpose(1, 0, 2).reshape(projector.shape).astype(jnp.float32)
    projector_new = projector_wide + eta_step * (
        math.sqrt(depth) * gram_rows / live_total - ridge_weight * projector_wide
    )
    return (targets_out, projector_new)


def solution(mesh):
    in_specs = (
        P("seq", "tp"),
        P("seq", "tp"),
        P("seq", "tp"),
        P("seq"),
        P("seq", None),
        P("seq", "tp"),
        P("seq"),
        P("seq"),
        P(),
    )
    out_specs = (P("seq", "tp"), P("seq", "tp"))
    return jax.shard_map(shards, mesh=mesh, in_specs=in_specs, out_specs=out_specs, check_vma=False)
```

```python
import functools
import math

import jax
import jax.numpy as jnp
from jax import lax
from jax.experimental import pallas as pl
from jax.experimental.pallas import tpu as pltpu
from jax.sharding import PartitionSpec as P

HD = 128
MAXSPAN = 4
RIM = 16

eta_step = 0.5
ridge_weight = 0.1
norm_eps = 1e-06
neg_large = -1e30

NT = (((1,), (1,)), ((), ()))


def attention_kernel(groups, spot_ref, q_ref, k_ref, v_ref, start_ref, hot_ref, out_ref,
                     acc, top, total, bias):
    own = spot_ref[0]
    lowest = spot_ref[1]
    tok = q_ref.shape[0]
    rate = HD ** (-0.5) * math.log2(math.e)
    top[...] = jnp.full(top.shape, neg_large, jnp.float32)
    total[...] = jnp.zeros(total.shape, jnp.float32)
    acc[...] = jnp.zeros(acc.shape, jnp.float32)
    query_pos = own * tok + lax.broadcasted_iota(jnp.int32, (tok, tok), 1)

    def meet(block, masked):
        key_block = k_ref[block, :tok, :]
        value_block = jnp.concatenate(
            [v_ref[block, r:r + HD, :] for r in range(0, tok, HD)], axis=1
        )
        for g in range(groups):
            lanes = slice(g * HD, (g + 1) * HD)
            scores = lax.dot_general(
                key_block, q_ref[:, lanes], NT, preferred_element_type=jnp.float32
            )
            if masked:
                scores = scores + bias[...]
            old_top = top[g:g + 1, :]
            new_top = jnp.maximum(old_top, jnp.max(scores, axis=0, keepdims=True))
            weights = jnp.exp2((scores - new_top) * rate)
            factor = jnp.exp2((old_top - new_top) * rate)
            top[g:g + 1, :] = new_top
            total[g:g + 1, :] = total[g:g + 1, :] * factor + jnp.sum(
                weights, axis=0, keepdims=True
            )
            acc[lanes, :] = acc[lanes, :] * factor + jnp.dot(
                value_block, weights.astype(jnp.bfloat16), preferred_element_type=jnp.float32
            )

    def advance(step, carry):
        block = own - step
        whole = (step > 0) & (block * tok >= spot_ref[2])

        @pl.when(whole)
        def _():
            meet(block, False)

        @pl.when(jnp.logical_not(whole))
        def _():
            key_pos = block * tok + lax.broadcasted_iota(jnp.int32, (tok, tok), 0)
            visible = (key_pos >= start_ref[...]) & (key_pos <= query_pos)
            bias[...] = jnp.where(visible, 0.0, neg_large)
            meet(block, True)

        return carry

    lax.fori_loop(0, own - lowest + 1, advance, 0)
    for g in range(groups):
        lanes = slice(g * HD, (g + 1) * HD)
        mixed = (acc[lanes, :] / total[g:g + 1, :]).astype(jnp.bfloat16)
        out_ref[:, lanes] = lax.dot_general(
            hot_ref[...], mixed, NT, preferred_element_type=jnp.float32
        )


def attend(spot, queries, mixed_blocks, doc_start, one_hot, kv_heads, groups):
    tok = queries.shape[0]
    count, rows = mixed_blocks.shape[:2]
    hot_rows = one_hot.shape[0]
    wide = groups * HD
    return pl.pallas_call(
        functools.partial(attention_kernel, groups),
        out_shape=jax.ShapeDtypeStruct((hot_rows, queries.shape[1]), jnp.float32),
        grid_spec=pltpu.PrefetchScalarGridSpec(
            num_scalar_prefetch=1,
            grid=(kv_heads,),
            in_specs=[
                pl.BlockSpec((tok, wide), lambda i, s: (0, i)),
                pl.BlockSpec((count, rows, HD), lambda i, s: (0, 0, i)),
                pl.BlockSpec((count, rows, HD), lambda i, s: (0, 0, i + kv_heads)),
                pl.BlockSpec((1, tok), lambda i, s: (0, 0)),
                pl.BlockSpec((hot_rows, tok), lambda i, s: (0, 0)),
            ],
            out_specs=pl.BlockSpec((hot_rows, wide), lambda i, s: (0, i)),
            scratch_shapes=[
                pltpu.VMEM((wide, tok), jnp.float32),
                pltpu.VMEM((groups, tok), jnp.float32),
                pltpu.VMEM((groups, tok), jnp.float32),
                pltpu.VMEM((tok, tok), jnp.float32),
            ],
        ),
        compiler_params=pltpu.CompilerParams(vmem_limit_bytes=40 * 1024 * 1024),
        cost_estimate=pl.CostEstimate(
            flops=4 * tok * queries.shape[1] * 2304,
            bytes_accessed=mixed_blocks.size * 2 + queries.size * 2,
            transcendentals=tok * queries.shape[1] // HD * 2304,
        ),
    )(spot, queries, mixed_blocks, mixed_blocks, doc_start, one_hot)


def step_kernel(depth, total_ref, old_ref, gram_ref, new_ref):
    wide = old_ref[...].astype(jnp.float32)
    gram = jnp.concatenate([gram_ref[i] for i in range(gram_ref.shape[0])], axis=1)
    gram = gram.astype(jnp.float32)
    rate = eta_step * math.sqrt(depth) / total_ref[...]
    new_ref[...] = wide * (1.0 - eta_step * ridge_weight) + gram * rate


def step(projector, gram_sum, live_total, depth):
    pieces, rows, chunk = gram_sum.shape
    return pl.pallas_call(
        functools.partial(step_kernel, depth),
        out_shape=jax.ShapeDtypeStruct(projector.shape, jnp.float32),
        grid=(pieces // 4,),
        in_specs=[
            pl.BlockSpec((1, 1), lambda i: (0, 0)),
            pl.BlockSpec((rows, 4 * chunk), lambda i: (0, i)),
            pl.BlockSpec((4, rows, chunk), lambda i: (i, 0, 0)),
        ],
        out_specs=pl.BlockSpec((rows, 4 * chunk), lambda i: (0, i)),
        compiler_params=pltpu.CompilerParams(vmem_limit_bytes=32 * 1024 * 1024),
    )(live_total.reshape(1, 1), projector, gram_sum)


def shards(queries, keys, values, doc_ids, features, projector, span_start, span_len, counts):
    tok = queries.shape[0]
    kv_heads = keys.shape[1] // HD
    groups = queries.shape[1] // (kv_heads * HD)
    slots = features.shape[0]
    tok_rows = projector.shape[0]
    seq_index = lax.axis_index("seq")
    seq_size = lax.axis_size("seq")
    first_row = seq_index * tok

    tp_size = lax.axis_size("tp")
    tp_index = lax.axis_index("tp")
    wide = 2 * keys.shape[1]
    doc_rows = jnp.zeros((RIM, wide), jnp.bfloat16)
    doc_rows = lax.dynamic_update_slice(doc_rows, doc_ids.astype(jnp.bfloat16)[None, :], (0, 0))
    turned = values.reshape(tok // HD, HD, kv_heads, HD).transpose(0, 3, 2, 1).reshape(keys.shape)
    mixed = jnp.concatenate([jnp.concatenate([keys, turned], axis=1), doc_rows], axis=0)
    mixed_blocks = lax.all_gather(mixed, "seq")
    all_docs = mixed_blocks[:, tok, :tok].reshape(-1).astype(jnp.int32)
    depth = features.shape[1]
    if tp_size == 2:
        half = depth // 2
        part = lax.dynamic_slice_in_dim(features, tp_index * half, half, axis=1)
    else:
        part = features
    part, projector_late, mixed_blocks = lax.optimization_barrier((part, projector, mixed_blocks))
    near = lax.all_gather(part, "seq", axis=0, tiled=True)
    chunk = projector.shape[1] // seq_size
    columns = lax.all_to_all(
        projector_late.reshape(tok_rows, seq_size, chunk).transpose(1, 0, 2), "seq", 0, 0
    ).reshape(depth, chunk)

    doc_start = jnp.sum((all_docs[None, :] < doc_ids[:, None]).astype(jnp.int32), axis=1)
    spot = jnp.stack([seq_index.astype(jnp.int32), doc_start[0] // tok, doc_start[tok - 1]])
    offsets = span_start - first_row
    places = jnp.arange(tok + RIM, dtype=jnp.int32)
    one_hot = (
        (places[None, :] >= offsets[:, None]) & (places[None, :] < (offsets + span_len)[:, None])
    ).astype(jnp.bfloat16)
    picks = (jnp.arange(RIM)[:, None] == jnp.arange(tok)[None, :]).astype(jnp.bfloat16)
    hot = jnp.concatenate([one_hot[:, :tok], picks], axis=0)
    pooled = attend(
        spot, queries, mixed_blocks, doc_start[None, :], hot, kv_heads, groups
    )
    columns, pooled = lax.optimization_barrier((columns, pooled))
    route = [(i + 1, i) for i in range(seq_size - 1)]
    rim = lax.ppermute(pooled[slots:].astype(jnp.bfloat16), "seq", route)
    span_sum = pooled[:slots] + jnp.dot(
        one_hot[:, tok:], rim, preferred_element_type=jnp.float32
    )
    is_live = jnp.arange(slots, dtype=jnp.int32) < lax.dynamic_index_in_dim(
        counts, seq_index, keepdims=False
    )
    span_mean = jnp.where(is_live[:, None], span_sum / span_len[:, None].astype(jnp.float32), 0.0)
    row_sq = lax.psum(jnp.sum(span_mean * span_mean, axis=1), "tp")
    mean_sq = row_sq / (span_mean.shape[1] * lax.axis_size("tp"))
    targets = (span_mean * lax.rsqrt(mean_sq + norm_eps)[:, None]).astype(jnp.bfloat16)

    near, targets_out = lax.optimization_barrier((near, targets))
    all_live = jnp.arange(slots, dtype=jnp.int32)[None, :] < counts[:, None]
    if tp_size == 2:
        far = lax.ppermute(near, "tp", [(0, 1), (1, 0)])
        near_rows = lax.dynamic_slice_in_dim(columns, tp_index * half, half, axis=0)
        far_rows = lax.dynamic_slice_in_dim(columns, (1 - tp_index) * half, half, axis=0)
        prediction = jnp.dot(near, near_rows, preferred_element_type=jnp.float32) + jnp.dot(
            far, far_rows, preferred_element_type=jnp.float32
        )
    else:
        prediction = jnp.dot(near, columns, preferred_element_type=jnp.float32)
    prediction = lax.optimization_barrier(prediction * depth ** (-0.5))
    target_columns = lax.all_to_all(
        targets.reshape(slots, seq_size, chunk).transpose(1, 0, 2), "seq", 0, 0
    )
    errors = jnp.where(
        all_live[:, :, None],
        target_columns.astype(jnp.float32) - prediction.reshape(seq_size, slots, chunk),
        0.0,
    ).astype(jnp.bfloat16)
    errors = lax.optimization_barrier(errors).reshape(seq_size * slots, chunk)
    over_slots = (((0,), (0,)), ((), ()))
    gram = lax.dot_general(near, errors, over_slots, preferred_element_type=jnp.float32).astype(
        jnp.bfloat16
    )
    if tp_size == 2:
        other = lax.dot_general(
            far, errors, over_slots, preferred_element_type=jnp.float32
        ).astype(jnp.bfloat16)
        first = tp_index == 0
        gram = jnp.concatenate([jnp.where(first, gram, other), jnp.where(first, other, gram)], 0)
    gram_sum = lax.all_to_all(gram.reshape(seq_size, tok_rows, chunk), "seq", 0, 0)
    live_total = jnp.sum(counts).astype(jnp.float32)
    if chunk % 128 == 0 and seq_size % 4 == 0:
        return (targets_out, step(projector, gram_sum, live_total, depth))
    projector_wide = projector.astype(jnp.float32)
    gram_rows = gram_sum.transpose(1, 0, 2).reshape(projector.shape).astype(jnp.float32)
    projector_new = projector_wide + eta_step * (
        math.sqrt(depth) * gram_rows / live_total - ridge_weight * projector_wide
    )
    return (targets_out, projector_new)


def solution(mesh):
    in_specs = (
        P("seq", "tp"),
        P("seq", "tp"),
        P("seq", "tp"),
        P("seq"),
        P("seq", None),
        P("seq", "tp"),
        P("seq"),
        P("seq"),
        P(),
    )
    out_specs = (P("seq", "tp"), P("seq", "tp"))
    return jax.shard_map(shards, mesh=mesh, in_specs=in_specs, out_specs=out_specs, check_vma=False)
```
